32 devices in a mesh: dp: 4 (over x, core), tensor: 8 (over z, y).
Axes of the slice: x: 2, y: 2, z: 4, core: 2. Of those that a mesh axis runs over, the one named last changes fastest.
Arguments:
- tokens: bfloat16 [2048, 8192], P('dp', 'tensor'), may hold values from -6 to 6
- first_right: bfloat16 [32, 256, 1024], P('tensor'), may hold values from -0.375 to 0.375
- first_left: bfloat16 [128, 256, 256], P('tensor'), may hold values from -0.375 to 0.375
- second_right: bfloat16 [128, 256, 256], P('tensor'), may hold values from -0.375 to 0.375
- second_left: bfloat16 [32, 1024, 256], P('tensor'), may hold values from -0.1875 to 0.1875
- cotangent: bfloat16 [2048, 8192], P('dp', 'tensor'), may hold values from -6 to 6
Outputs:
- layer_out: bfloat16 [2048, 8192], P('dp', 'tensor')
- grad_tokens: bfloat16 [2048, 8192], P('dp', 'tensor')
- grad_first_right: float32 [32, 256, 1024], P('tensor', 'dp')
- grad_first_left: float32 [128, 256, 256], P('tensor', 'dp')
- grad_second_right: float32 [128, 256, 256], P('tensor', 'dp')
- grad_second_left: float32 [32, 1024, 256], P('tensor', 'dp')
The draws below stay inside these ranges and needn't reach their ends.
All inputs are finite; a program needn't handle non-finite values.
Results may differ from the reference program's by a relative error of at most 0.018.
Values may be sent and summed in bfloat16 or wider, within the bound.
A program may use at most 128 MiB of HBM per device.

```python
import jax
import jax.numpy as jnp
from jax import lax

D = 8192
BLK = 256
TOK_DEV = 512
NB_IN = 32
NB_HID = 128
WIDE = 1024
SUB = 8
TOKENS = 2048
N_DP = 4


def block_levels(rng, shape, pieces, smallest, top_value):
    def one(position, blocks):
        draws = jax.random.uniform(jax.random.fold_in(jax.random.fold_in(rng, 6), position), (blocks,), jnp.float32, smallest / len(pieces), top_value / len(pieces))
        return jnp.repeat(jnp.exp(draws), shape[position] // blocks).reshape((-1,) + (1,) * (len(shape) - position - 1))

    level = one(*pieces[0])
    for cut in pieces[1:]:
        level = level * one(*cut)
    return level


def normal_values(rng, extent, scale, reach, split=(), dtype=jnp.bfloat16):
    drawn = scale * jax.random.normal(rng, extent, jnp.float32)
    if split:
        drawn = drawn * block_levels(rng, extent, split, -0.22, 0.18)
    return jnp.clip(drawn, -reach, reach).astype(dtype)


def setup_inputs(seed: int = 0) -> dict:
    seeds = jax.random.split(jax.random.key(seed), 7)
    return {
        "tokens": normal_values(seeds[0], (TOKENS, D), 1.0, 6.0, ((0, 4), (1, 8))),
        "first_right": normal_values(seeds[1], (NB_IN, BLK, WIDE), BLK ** -0.5, 0.375, ((0, 8),)),
        "first_left": normal_values(seeds[2], (NB_HID, BLK, BLK), BLK ** -0.5, 0.375, ((0, 8),)),
        "second_right": normal_values(seeds[3], (NB_HID, BLK, BLK), BLK ** -0.5, 0.375, ((0, 8),)),
        "second_left": normal_values(seeds[4], (NB_IN, WIDE, BLK), WIDE ** -0.5, 0.1875, ((0, 8),)),
        "cotangent": normal_values(seeds[5], (TOKENS, D), 1.0, 6.0, ((0, 4), (1, 8))),
    }


half_root = 0.7071067811865476
inv_root_two_pi = 0.3989422804014327


def gelu_value(value):
    return 0.5 * value * (1.0 + jax.scipy.special.erf(value * half_root))


def gelu_slope(value):
    return 0.5 * (1.0 + jax.scipy.special.erf(value * half_root)) + value * jnp.exp(-0.5 * value * value) * inv_root_two_pi


def reference(tokens, first_right, first_left, second_right, second_left, cotangent):
    fp = jnp.float32
    bf = jnp.bfloat16
    grad_scale = float(TOKENS) ** -0.5
    right_one = first_right.astype(fp).reshape(NB_IN, BLK, NB_HID, SUB)
    left_one = first_left.astype(fp)
    right_two = second_right.astype(fp).reshape(NB_HID, BLK, NB_IN, SUB)
    left_two = second_left.astype(fp)

    def one_block(carry, inputs):
        tok_block, cot_block = inputs
        tok_rows = tok_block.shape[0]
        tok_parts = tok_block.astype(fp).reshape(tok_rows, NB_IN, BLK)
        up_inner = jnp.einsum('tkb,kbjg->jtkg', tok_parts, right_one).astype(bf)
        mixed_up = up_inner.reshape(NB_HID, tok_rows, BLK).astype(fp)
        pre_act = jnp.einsum('jtb,jbc->jtc', mixed_up, left_one)
        hidden = gelu_value(pre_act).astype(bf).astype(fp)
        down_inner = jnp.einsum('jtb,jbkg->ktjg', hidden, right_two).astype(bf)
        mixed_down = down_inner.reshape(NB_IN, tok_rows, WIDE).astype(fp)
        out_block = jnp.einsum('ktw,kwc->tkc', mixed_down, left_two).astype(bf).reshape(tok_rows, D)
        cot_parts = cot_block.astype(fp).reshape(tok_rows, NB_IN, BLK)
        d_mixed_down = jnp.einsum('tkc,kwc->ktw', cot_parts, left_two).astype(bf).astype(fp)
        d_down_inner = d_mixed_down.reshape(NB_IN, tok_rows, NB_HID, SUB)
        d_hidden = jnp.einsum('ktjg,jbkg->jtb', d_down_inner, right_two)
        d_pre = (d_hidden * gelu_slope(pre_act)).astype(bf).astype(fp)
        d_mixed_up = jnp.einsum('jtc,jbc->jtb', d_pre, left_one).astype(bf).astype(fp)
        d_up_inner = d_mixed_up.reshape(NB_HID, tok_rows, NB_IN, SUB)
        grad_block = jnp.einsum('jtkg,kbjg->tkb', d_up_inner, right_one).astype(bf).reshape(tok_rows, D)
        grad_left_two = jnp.einsum('ktw,tkc->kwc', mixed_down, cot_parts) * grad_scale
        grad_right_two = jnp.einsum('jtb,ktjg->jbkg', hidden, d_down_inner).reshape(NB_HID, BLK, BLK) * grad_scale
        grad_left_one = jnp.einsum('jtb,jtc->jbc', mixed_up, d_pre) * grad_scale
        grad_right_one = jnp.einsum('tkb,jtkg->kbjg', tok_parts, d_up_inner).reshape(NB_IN, BLK, WIDE) * grad_scale
        totals = (carry[0] + grad_right_one, carry[1] + grad_left_one, carry[2] + grad_right_two, carry[3] + grad_left_two)
        return totals, (out_block, grad_block)

    start = (jnp.zeros((NB_IN, BLK, WIDE), fp), jnp.zeros((NB_HID, BLK, BLK), fp),
             jnp.zeros((NB_HID, BLK, BLK), fp), jnp.zeros((NB_IN, WIDE, BLK), fp))
    tok_split = tokens.reshape(N_DP, TOK_DEV, D)
    cot_split = cotangent.reshape(N_DP, TOK_DEV, D)
    totals, stacked = lax.scan(one_block, start, (tok_split, cot_split))
    layer_out = stacked[0].reshape(TOKENS, D)
    grad_tokens = stacked[1].reshape(TOKENS, D)
    return layer_out, grad_tokens, totals[0], totals[1], totals[2], totals[3]
```

```python
import jax
import jax.numpy as jnp
from jax import lax
from jax.sharding import PartitionSpec as P

half_root = 0.7071067811865476
inv_root_two_pi = 0.3989422804014327
fp = jnp.float32
bf = jnp.bfloat16


def gelu_value(value):
    return 0.5 * value * (1.0 + jax.scipy.special.erf(value * half_root))


def gelu_slope(value):
    return (
        0.5 * (1.0 + jax.scipy.special.erf(value * half_root))
        + value * jnp.exp(-0.5 * value * value) * inv_root_two_pi
    )


def dot(spec, left, right):
    return jnp.einsum(spec, left, right, preferred_element_type=fp)


def shards(tokens, first_right, first_left, second_right, second_left, cotangent):
    tok_rows = tokens.shape[0]
    in_blocks, block_width, wide_width = first_right.shape
    hid_blocks = first_left.shape[0]
    groups = lax.axis_size("tensor")
    replicas = lax.axis_size("dp")
    members = groups // 2
    half_in = in_blocks * members
    half_hid = hid_blocks * members
    half_wide = wide_width // 2
    sub_width = wide_width // (half_hid * 2)
    half_rows = half_in * sub_width
    grad_scale = float(tok_rows * replicas) ** (-0.5)
    me = lax.axis_index("tensor")
    place = lax.axis_index("dp")
    half = me // members
    other = 1 - half
    swap = [(i, (i + members) % groups) for i in range(groups)]
    teams = [list(range(members)), list(range(members, groups))]

    def to_partner(value):
        return lax.ppermute(value, "tensor", swap)

    def within(value, split, concat):
        return lax.all_to_all(
            value, "tensor", split_axis=split, concat_axis=concat, axis_index_groups=teams, tiled=True
        )

    def cut(value, which, axis):
        size = value.shape[axis] // 2
        return lax.dynamic_slice_in_dim(value, which * size, size, axis)

    def join(mine, theirs, axis):
        return jnp.where(
            half == 0,
            jnp.concatenate([mine, theirs], axis),
            jnp.concatenate([theirs, mine], axis),
        )

    def factor_of_partner(value):
        rows = value.shape[1] // replicas
        part = lax.dynamic_slice_in_dim(value, place * rows, rows, 1)
        return lax.all_gather(to_partner(part), "dp", axis=1, tiled=True)

    def scatter_sum(value):
        return lax.psum_scatter((value * grad_scale).astype(bf), "dp", scatter_dimension=0, tiled=True)

    right_mine = cut(first_right, half, 2)
    right_theirs = factor_of_partner(cut(first_right, other, 2))
    tok_theirs = to_partner(tokens)
    last_mine = cut(second_left, half, 1)
    last_theirs = factor_of_partner(cut(second_left, other, 1))
    cot_theirs = to_partner(cotangent)

    def blocks(value):
        return value.reshape(tok_rows, in_blocks, block_width)

    def split_right(value):
        return value.reshape(in_blocks, block_width, half_hid, sub_width)

    left_one = jnp.concatenate([cut(first_left, half, 1), cut(first_left, other, 1)], 1)
    right_two = jnp.concatenate([cut(second_right, half, 2), cut(second_right, other, 2)], 2)
    right_two_mine = right_two[:, :, :half_rows].reshape(hid_blocks, block_width, half_in, sub_width)
    right_two_theirs = right_two[:, :, half_rows:].reshape(
        hid_blocks, block_width, half_in, sub_width
    )

    def up(tok, right):
        inner = dot("tkb,kbjg->jkgt", blocks(tok), split_right(right)).astype(bf)
        return within(inner, 0, 1).reshape(hid_blocks, half_rows, tok_rows)

    def up_cot(cot, last):
        last = last.reshape(in_blocks, half_hid, sub_width, block_width)
        inner = dot("tkc,kjgc->jkgt", blocks(cot), last).astype(bf)
        return within(inner, 0, 1).reshape(hid_blocks, half_rows, tok_rows)

    up_mine = up(tokens, right_mine)
    cot_mine = up_cot(cotangent, last_mine)
    up_theirs = up(tok_theirs, right_theirs)
    mixed_up = jnp.concatenate([up_mine, up_theirs], 1)
    pre_piece = dot("jbt,jbc->jct", mixed_up, left_one)
    hidden = gelu_value(pre_piece).astype(bf)

    def down(right):
        inner = dot("jbt,jbkg->kjgt", hidden, right).astype(bf)
        return within(inner, 0, 1).reshape(in_blocks, half_wide, tok_rows)

    down_theirs = down(right_two_theirs)
    down_mine = down(right_two_mine)

    d_down = jnp.concatenate([cot_mine, up_cot(cot_theirs, last_theirs)], 1)
    d_hidden = dot("jrt,jbr->jbt", d_down, right_two)
    d_pre = (d_hidden * gelu_slope(pre_piece)).astype(bf)

    def back(left):
        inner = dot("jct,jkgc->kjgt", d_pre, left.reshape(hid_blocks, half_in, sub_width, block_width))
        return within(inner.astype(bf), 0, 1).reshape(in_blocks, half_wide, tok_rows)

    d_up_theirs = back(left_one[:, half_rows:])
    d_up_mine = back(left_one[:, :half_rows])

    def together(mine, theirs):
        theirs = to_partner(theirs.astype(bf).reshape(tok_rows, in_blocks * block_width))
        return (mine.reshape(theirs.shape) + theirs.astype(fp)).astype(bf)

    layer_out = together(
        dot("kwt,kwc->tkc", down_mine, last_mine), dot("kwt,kwc->tkc", down_theirs, last_theirs)
    )
    grad_tokens = together(
        dot("kwt,kbw->tkb", d_up_mine, right_mine), dot("kwt,kbw->tkb", d_up_theirs, right_theirs)
    )

    two = dot("jbt,jrt->bjr", hidden, d_down)
    grad_right_two = scatter_sum(join(two[:, :, :half_rows], two[:, :, half_rows:], 2))
    one = dot("jrt,jct->rjc", mixed_up, d_pre)
    grad_left_one = scatter_sum(join(one[:half_rows], one[half_rows:], 0))

    last = scatter_sum(
        join(
            dot("kwt,tkc->wkc", down_mine, blocks(cotangent)),
            dot("kwt,tkc->wkc", down_theirs, blocks(cot_theirs)),
            0,
        )
    )
    near = replicas // 2
    pairs = []
    for d in range(replicas):
        for m in range(groups):
            if d // near != m // members:
                source = d * groups + m
                pairs.append((source, ((d + near) % replicas) * groups + (m + members) % groups))
    came = lax.ppermute(last, ("dp", "tensor"), pairs)
    grad_left_two = jnp.where(place // near == half, last, came)

    right_sum_theirs = to_partner(
        scatter_sum(dot("tkb,kwt->bkw", blocks(tok_theirs), d_up_theirs))
    )
    right_sum_mine = scatter_sum(dot("tkb,kwt->bkw", blocks(tokens), d_up_mine))
    grad_right_one = join(right_sum_mine, right_sum_theirs, 2)

    def last_form(value):
        return jnp.transpose(value.astype(fp), (1, 0, 2))

    return (
        layer_out,
        grad_tokens,
        last_form(grad_right_one),
        last_form(grad_left_one),
        last_form(grad_right_two),
        last_form(grad_left_two),
    )


def solution(mesh):
    in_specs = (
        P("dp", "tensor"),
        P("tensor", None, None),
        P("tensor", None, None),
        P("tensor", None, None),
        P("tensor", None, None),
        P("dp", "tensor"),
    )
    out_specs = (
        P("dp", "tensor"),
        P("dp", "tensor"),
        P("tensor", "dp", None),
        P("tensor", "dp", None),
        P("tensor", "dp", None),
        P("tensor", "dp", None),
    )
    return jax.shard_map(shards, mesh=mesh, in_specs=in_specs, out_specs=out_specs, check_vma=False)
```

```python
import jax
import jax.numpy as jnp
from jax import lax
from jax.sharding import PartitionSpec as P

half_root = 0.7071067811865476
inv_root_two_pi = 0.3989422804014327
fp = jnp.float32
bf = jnp.bfloat16


def gelu_value(value):
    return 0.5 * value * (1.0 + jax.scipy.special.erf(value * half_root))


def gelu_slope(value):
    return (
        0.5 * (1.0 + jax.scipy.special.erf(value * half_root))
        + value * jnp.exp(-0.5 * value * value) * inv_root_two_pi
    )


def dot(spec, left, right):
    return jnp.einsum(spec, left, right, preferred_element_type=fp)


def after(value, *others):
    return lax.optimization_barrier((value, *others))[0]


def shards(tokens, first_right, first_left, second_right, second_left, cotangent):
    tok_rows = tokens.shape[0]
    in_blocks, block_width, wide_width = first_right.shape
    hid_blocks = first_left.shape[0]
    groups = lax.axis_size("tensor")
    replicas = lax.axis_size("dp")
    members = groups // 2
    half_in = in_blocks * members
    half_hid = hid_blocks * members
    half_wide = wide_width // 2
    sub_width = wide_width // (half_hid * 2)
    half_rows = half_in * sub_width
    grad_scale = float(tok_rows * replicas) ** (-0.5)
    me = lax.axis_index("tensor")
    place = lax.axis_index("dp")
    half = me // members
    other = 1 - half
    swap = [(i, (i + members) % groups) for i in range(groups)]
    teams = [list(range(members)), list(range(members, groups))]

    def to_partner(value):
        return lax.ppermute(value, "tensor", swap)

    def within(value, split, concat):
        return lax.all_to_all(
            value, "tensor", split_axis=split, concat_axis=concat, axis_index_groups=teams, tiled=True
        )

    def cut(value, which, axis):
        size = value.shape[axis] // 2
        return lax.dynamic_slice_in_dim(value, which * size, size, axis)

    def join(mine, theirs, axis):
        return jnp.where(
            half == 0,
            jnp.concatenate([mine, theirs], axis),
            jnp.concatenate([theirs, mine], axis),
        )

    def factor_of_partner(value):
        rows = value.shape[1] // replicas
        part = lax.dynamic_slice_in_dim(value, place * rows, rows, 1)
        return lax.all_gather(to_partner(part), "dp", axis=1, tiled=True)

    def scaled(value):
        return (value * grad_scale).astype(bf)

    def scatter(value):
        return lax.psum_scatter(value, "dp", scatter_dimension=0, tiled=True)

    def scatter_sum(value):
        return scatter(scaled(value))

    right_mine = cut(first_right, half, 2)
    right_theirs = factor_of_partner(cut(first_right, other, 2))
    tok_theirs = to_partner(tokens)
    last_mine = cut(second_left, half, 1)
    last_theirs = factor_of_partner(cut(second_left, other, 1))
    cot_theirs = to_partner(after(cotangent, tok_theirs))

    def blocks(value):
        return value.reshape(tok_rows, in_blocks, block_width)

    def split_right(value):
        return value.reshape(in_blocks, block_width, half_hid, sub_width)

    left_one = jnp.concatenate([cut(first_left, half, 1), cut(first_left, other, 1)], 1)
    right_two = jnp.concatenate([cut(second_right, half, 2), cut(second_right, other, 2)], 2)
    right_two_mine = right_two[:, :, :half_rows].reshape(hid_blocks, block_width, half_in, sub_width)
    right_two_theirs = right_two[:, :, half_rows:].reshape(
        hid_blocks, block_width, half_in, sub_width
    )

    def up(tok, right, *first):
        inner = dot("tkb,kbjg->jkgt", blocks(tok), split_right(right)).astype(bf)
        inner = after(inner, *first)
        return within(inner, 0, 1).reshape(hid_blocks, half_rows, tok_rows)

    def up_cot(cot, last, *first):
        last = last.reshape(in_blocks, half_hid, sub_width, block_width)
        inner = dot("tkc,kjgc->jkgt", blocks(cot), last).astype(bf)
        inner = after(inner, *first)
        return within(inner, 0, 1).reshape(hid_blocks, half_rows, tok_rows)

    up_mine = up(tokens, right_mine)
    cot_mine = up_cot(cotangent, last_mine, up_mine)
    up_theirs = up(tok_theirs, right_theirs, cot_mine)
    d_down_theirs = up_cot(cot_theirs, last_theirs, up_theirs)
    mixed_up = jnp.concatenate([up_mine, up_theirs], 1)
    pre_piece = dot("jbt,jbc->jct", mixed_up, left_one)
    hidden = gelu_value(pre_piece).astype(bf)

    def down(right, *first):
        inner = dot("jbt,jbkg->kjgt", hidden, right).astype(bf)
        inner = after(inner, *first)
        return within(inner, 0, 1).reshape(in_blocks, half_wide, tok_rows)

    def back(left, *first):
        inner = dot("jct,jkgc->kjgt", d_pre, left.reshape(hid_blocks, half_in, sub_width, block_width))
        inner = after(inner.astype(bf), *first)
        return within(inner, 0, 1).reshape(in_blocks, half_wide, tok_rows)

    def cross(theirs):
        return to_partner(theirs.astype(bf).reshape(tok_rows, in_blocks * block_width))

    def together(mine, came):
        return (mine.reshape(came.shape) + came.astype(fp)).astype(bf)

    down_theirs = down(right_two_theirs, d_down_theirs)
    layer_came = cross(dot("kwt,kwc->tkc", down_theirs, last_theirs))

    d_down = jnp.concatenate([cot_mine, d_down_theirs], 1)
    d_hidden = dot("jrt,jbr->jbt", d_down, right_two)
    d_pre = (d_hidden * gelu_slope(pre_piece)).astype(bf)

    two = dot("jbt,jrt->bjr", hidden, d_down)
    two = scaled(join(two[:, :, :half_rows], two[:, :, half_rows:], 2))
    one = dot("jrt,jct->rjc", mixed_up, d_pre)
    one = scaled(join(one[:half_rows], one[half_rows:], 0))

    d_up_theirs = back(left_one[:, half_rows:], down_theirs, one, two)
    grad_left_one = scatter(one)
    grad_right_two = scatter(two)
    grad_came = cross(dot("kwt,kbw->tkb", d_up_theirs, right_theirs))
    down_mine = down(right_two_mine, d_up_theirs, layer_came)
    d_up_mine = back(left_one[:, :half_rows], down_mine, grad_came, grad_left_one)

    layer_out = together(dot("kwt,kwc->tkc", down_mine, last_mine), layer_came)
    grad_tokens = together(dot("kwt,kbw->tkb", d_up_mine, right_mine), grad_came)

    last = scatter_sum(
        join(
            dot("kwt,tkc->wkc", down_mine, blocks(cotangent)),
            dot("kwt,tkc->wkc", down_theirs, blocks(cot_theirs)),
            0,
        )
    )
    near = replicas // 2
    pairs = []
    for d in range(replicas):
        for m in range(groups):
            if d // near != m // members:
                source = d * groups + m
                pairs.append((source, ((d + near) % replicas) * groups + (m + members) % groups))
    came = lax.ppermute(last, ("dp", "tensor"), pairs)
    grad_left_two = jnp.where(place // near == half, last, came)

    right_sum_theirs = to_partner(
        scatter_sum(dot("tkb,kwt->bkw", blocks(tok_theirs), d_up_theirs))
    )
    right_sum_mine = scatter_sum(dot("tkb,kwt->bkw", blocks(tokens), d_up_mine))
    grad_right_one = join(right_sum_mine, right_sum_theirs, 2)

    def last_form(value):
        return jnp.transpose(value.astype(fp), (1, 0, 2))

    return (
        layer_out,
        grad_tokens,
        last_form(grad_right_one),
        last_form(grad_left_one),
        last_form(grad_right_two),
        last_form(grad_left_two),
    )


def solution(mesh):
    in_specs = (
        P("dp", "tensor"),
        P("tensor", None, None),
        P("tensor", None, None),
        P("tensor", None, None),
        P("tensor", None, None),
        P("dp", "tensor"),
    )
    out_specs = (
        P("dp", "tensor"),
        P("dp", "tensor"),
        P("tensor", "dp", None),
        P("tensor", "dp", None),
        P("tensor", "dp", None),
        P("tensor", "dp", None),
    )
    return jax.shard_map(shards, mesh=mesh, in_specs=in_specs, out_specs=out_specs, check_vma=False)
```

```python
import jax
import jax.numpy as jnp
from jax import lax
from jax.sharding import PartitionSpec as P

half_root = 0.7071067811865476
inv_root_two_pi = 0.3989422804014327
fp = jnp.float32
bf = jnp.bfloat16


def gelu_value(value):
    return 0.5 * value * (1.0 + jax.scipy.special.erf(value * half_root))


def gelu_slope(value):
    return (
        0.5 * (1.0 + jax.scipy.special.erf(value * half_root))
        + value * jnp.exp(-0.5 * value * value) * inv_root_two_pi
    )


def dot(spec, left, right):
    return jnp.einsum(spec, left, right, preferred_element_type=fp)


def after(value, *others):
    for item in others:
        first = lax.slice(item, (0,) * item.ndim, (1,) * item.ndim).reshape(())
        value = value + (first * jnp.zeros((), first.dtype)).astype(value.dtype)
    return value


def shards(tokens, first_right, first_left, second_right, second_left, cotangent):
    tok_rows = tokens.shape[0]
    in_blocks, block_width, wide_width = first_right.shape
    hid_blocks = first_left.shape[0]
    groups = lax.axis_size("tensor")
    replicas = lax.axis_size("dp")
    members = groups // 2
    half_in = in_blocks * members
    half_hid = hid_blocks * members
    all_in = in_blocks * groups
    sub_width = wide_width // (half_hid * 2)
    half_rows = half_in * sub_width
    grad_scale = float(tok_rows * replicas) ** (-0.5)
    me = lax.axis_index("tensor")
    place = lax.axis_index("dp")
    half = me // members
    other = 1 - half
    swap = [(i, (i + members) % groups) for i in range(groups)]
    teams = [list(range(members)), list(range(members, groups))]

    def to_partner(value):
        return lax.ppermute(value, "tensor", swap)

    def within(value, split, concat):
        return lax.all_to_all(
            value, "tensor", split_axis=split, concat_axis=concat, axis_index_groups=teams, tiled=True
        )

    def cut(value, which, axis):
        size = value.shape[axis] // 2
        return lax.dynamic_slice_in_dim(value, which * size, size, axis)

    def join(mine, theirs, axis):
        return jnp.where(
            half == 0,
            jnp.concatenate([mine, theirs], axis),
            jnp.concatenate([theirs, mine], axis),
        )

    def part_of(value):
        rows = value.shape[1] // replicas
        return lax.dynamic_slice_in_dim(value, place * rows, rows, 1)

    def scaled(value):
        return (value * grad_scale).astype(bf)

    def scatter(value):
        return lax.psum_scatter(value, "dp", scatter_dimension=0, tiled=True)

    def scatter_sum(value):
        return scatter(scaled(value))

    right_mine = cut(first_right, half, 2)
    last_mine = cut(second_left, half, 1)
    right_part = part_of(cut(first_right, other, 2))
    last_part = part_of(cut(second_left, other, 1))
    parts = to_partner(jnp.concatenate([right_part.reshape(-1, 128), last_part.reshape(-1, 128)], 0))
    tok_theirs = to_partner(after(tokens, parts))
    edge = right_part.size // 128
    right_theirs = lax.all_gather(parts[:edge].reshape(right_part.shape), "dp", axis=1, tiled=True)
    last_theirs = lax.all_gather(parts[edge:].reshape(last_part.shape), "dp", axis=1, tiled=True)

    def blocks(value):
        return value.reshape(tok_rows, in_blocks, block_width)

    def split_right(value):
        return value.reshape(in_blocks, block_width, half_hid, sub_width)

    left_one = jnp.concatenate([cut(first_left, half, 1), cut(first_left, other, 1)], 1)
    right_two = jnp.concatenate([cut(second_right, half, 2), cut(second_right, other, 2)], 2)
    right_two_whole = second_right.reshape(hid_blocks, block_width, all_in, sub_width)
    left_one_whole = first_left.reshape(hid_blocks, all_in, sub_width, block_width)

    def up(tok, right):
        return dot("tkb,kbjg->jkgt", blocks(tok), split_right(right)).astype(bf)

    def up_cot(cot, last):
        last = last.reshape(in_blocks, half_hid, sub_width, block_width)
        return dot("tkc,kjgc->jkgt", blocks(cot), last).astype(bf)

    def rows(value):
        return value.reshape(hid_blocks, half_rows, tok_rows)

    up_mine = within(after(up(tokens, right_mine), parts), 0, 1)
    cot_mine = within(after(up_cot(cotangent, last_mine), up_mine), 0, 1)
    cot_theirs = to_partner(after(cotangent, tok_theirs, up_mine))
    up_theirs = within(after(up(tok_theirs, right_theirs), cot_mine), 0, 1)
    d_down_theirs = within(after(up_cot(cot_theirs, last_theirs), up_theirs), 0, 1)
    mixed_up = jnp.concatenate([rows(up_mine), rows(up_theirs)], 1)
    pre_piece = dot("jbt,jbc->jct", mixed_up, left_one)
    hidden = gelu_value(pre_piece).astype(bf)

    def home(value, *first):
        value = after(value.astype(bf), *first)
        value = lax.all_to_all(value, "tensor", split_axis=0, concat_axis=1, tiled=True)
        return value.reshape(in_blocks, wide_width, tok_rows)

    mixed_down = home(dot("jbt,jbkg->kjgt", hidden, right_two_whole), d_down_theirs)

    d_down = jnp.concatenate([rows(cot_mine), rows(d_down_theirs)], 1)
    d_hidden = dot("jrt,jbr->jbt", d_down, right_two)
    d_pre = (d_hidden * gelu_slope(pre_piece)).astype(bf)
    back = dot("jct,jkgc->kjgt", d_pre, left_one_whole)

    two = dot("jbt,jrt->bjr", hidden, d_down)
    two = scaled(join(two[:, :, :half_rows], two[:, :, half_rows:], 2))
    one = dot("jrt,jct->rjc", mixed_up, d_pre)
    one = scaled(join(one[:half_rows], one[half_rows:], 0))

    grad_left_one = scatter(one)
    grad_right_two = scatter(two)
    d_up = home(back, mixed_down, grad_left_one, grad_right_two)
    grad_left_two = scatter(scaled(dot("kwt,tkc->wkc", mixed_down, blocks(cotangent))))
    grad_right_one = scatter(scaled(dot("tkb,kwt->bkw", blocks(tokens), d_up)))

    def merged(value):
        return value.astype(bf).reshape(tok_rows, in_blocks * block_width)

    layer_out = merged(dot("kwt,kwc->tkc", mixed_down, second_left))
    grad_tokens = merged(dot("kwt,kbw->tkb", d_up, first_right))

    def last_form(value):
        return jnp.transpose(value.astype(fp), (1, 0, 2))

    return (
        layer_out,
        grad_tokens,
        last_form(grad_right_one),
        last_form(grad_left_one),
        last_form(grad_right_two),
        last_form(grad_left_two),
    )


def solution(mesh):
    in_specs = (
        P("dp", "tensor"),
        P("tensor", None, None),
        P("tensor", None, None),
        P("tensor", None, None),
        P("tensor", None, None),
        P("dp", "tensor"),
    )
    out_specs = (
        P("dp", "tensor"),
        P("dp", "tensor"),
        P("tensor", "dp", None),
        P("tensor", "dp", None),
        P("tensor", "dp", None),
        P("tensor", "dp", None),
    )
    return jax.shard_map(shards, mesh=mesh, in_specs=in_specs, out_specs=out_specs, check_vma=False)
```

```python
import jax
import jax.numpy as jnp
from jax import lax
from jax.sharding import PartitionSpec as P

half_root = 0.7071067811865476
inv_root_two_pi = 0.3989422804014327


def gelu_value(value):
    return 0.5 * value * (1.0 + jax.scipy.special.erf(value * half_root))


def gelu_slope(value):
    return (
        0.5 * (1.0 + jax.scipy.special.erf(value * half_root))
        + value * jnp.exp(-0.5 * value * value) * inv_root_two_pi
    )


def shards(tokens, first_right, first_left, second_right, second_left, cotangent):
    fp = jnp.float32
    bf = jnp.bfloat16
    tok_rows = tokens.shape[0]
    in_blocks, block_width, wide_width = first_right.shape
    hid_blocks = first_left.shape[0]
    groups = lax.axis_size("tensor")
    replicas = lax.axis_size("dp")
    all_in = in_blocks * groups
    all_hid = hid_blocks * groups
    sub_width = wide_width // all_hid
    grad_scale = float(tok_rows * replicas) ** (-0.5)
    right_one = first_right.reshape(in_blocks, block_width, all_hid, sub_width)
    right_two = second_right.reshape(hid_blocks, block_width, all_in, sub_width)
    tok_parts = tokens.reshape(tok_rows, in_blocks, block_width)
    cot_parts = cotangent.reshape(tok_rows, in_blocks, block_width)

    def dot(spec, left, right):
        return jnp.einsum(spec, left, right, preferred_element_type=fp)

    def exchange(value):
        return lax.all_to_all(value, "tensor", split_axis=0, concat_axis=1, tiled=True)

    def summed(value):
        lead, rows, width = value.shape
        value = (value * grad_scale).astype(bf)
        value = value.reshape(lead, replicas, rows // replicas, width)
        value = jnp.transpose(value, (1, 0, 2, 3))
        return lax.psum_scatter(value, "dp", scatter_dimension=0, tiled=False).astype(fp)

    arrived = exchange(dot("tkb,kbjg->jkgt", tok_parts, right_one).astype(bf))
    last_four = second_left.reshape(in_blocks, all_hid, sub_width, block_width)
    d_sent = dot("tkc,kjgc->jkgt", cot_parts, last_four).astype(bf)
    d_sent, arrived = lax.optimization_barrier((d_sent, arrived))
    d_arrived = exchange(d_sent)

    mixed_piece = arrived.reshape(hid_blocks, block_width, tok_rows)
    pre_piece = dot("jbt,jbc->jct", mixed_piece, first_left)
    hidden = gelu_value(pre_piece).astype(bf)
    down_sent = dot("jbt,jbkg->kjgt", hidden, right_two).astype(bf)
    down_sent, d_arrived = lax.optimization_barrier((down_sent, d_arrived))
    mixed_down = exchange(down_sent)

    d_down = d_arrived.reshape(hid_blocks, block_width, tok_rows)
    d_hidden = dot("jrt,jbr->jbt", d_down, second_right)
    d_pre = (d_hidden * gelu_slope(pre_piece)).astype(bf)

    pieces = 2 if in_blocks % 2 == 0 else 1
    part = in_blocks // pieces
    left_parts = first_left.reshape(hid_blocks, groups, in_blocks, sub_width, block_width)

    def back(place):
        left = left_parts[:, :, place * part : (place + 1) * part]
        left = left.reshape(hid_blocks, groups * part, sub_width, block_width)
        return dot("jct,jkgc->kjgt", d_pre, left).astype(bf)

    sent = [back(place) for place in range(pieces)]
    sent[0], mixed_down = lax.optimization_barrier((sent[0], mixed_down))
    grad_left_one = summed(dot("jbt,jct->jbc", mixed_piece, d_pre))
    grad_right_two = summed(dot("jbt,jrt->jbr", hidden, d_down))
    mixed_down = mixed_down.reshape(in_blocks, wide_width, tok_rows)

    token_parts = []
    sum_parts = []
    for place in range(pieces):
        d_up = exchange(sent[place])
        if place + 1 < pieces:
            sent[place + 1], d_up, grad_left_one, grad_right_two = lax.optimization_barrier(
                (sent[place + 1], d_up, grad_left_one, grad_right_two)
            )
        d_up = d_up.reshape(part, wide_width, tok_rows)
        chosen = slice(place * part, (place + 1) * part)
        sum_parts.append(summed(dot("tkb,kwt->kbw", tok_parts[:, chosen], d_up)))
        token_parts.append(dot("kwt,kbw->tkb", d_up, first_right[chosen]).astype(bf))
    grad_left_two = summed(dot("kwt,tkc->kwc", mixed_down, cot_parts))
    layer_out = dot("kwt,kwc->tkc", mixed_down, second_left).astype(bf)
    layer_out = layer_out.reshape(tok_rows, in_blocks * block_width)
    grad_tokens = jnp.concatenate(token_parts, 1).reshape(tok_rows, in_blocks * block_width)
    grad_right_one = jnp.concatenate(sum_parts, 0)
    return (layer_out, grad_tokens, grad_right_one, grad_left_one, grad_right_two, grad_left_two)


def solution(mesh):
    in_specs = (
        P("dp", "tensor"),
        P("tensor", None, None),
        P("tensor", None, None),
        P("tensor", None, None),
        P("tensor", None, None),
        P("dp", "tensor"),
    )
    out_specs = (
        P("dp", "tensor"),
        P("dp", "tensor"),
        P("tensor", "dp", None),
        P("tensor", "dp", None),
        P("tensor", "dp", None),
        P("tensor", "dp", None),
    )
    return jax.shard_map(shards, mesh=mesh, in_specs=in_specs, out_specs=out_specs, check_vma=False)
```
